32 devices in a mesh: rows: 4 (over x, core), chan: 2 (over y), filt: 4 (over z).
Axes of the slice: x: 2, y: 2, z: 4, core: 2. Of those that a mesh axis runs over, the one named last changes fastest.
Arguments:
- images: bfloat16 [16, 2048, 2048], P('rows', 'chan', 'filt'), may hold values from -6 to 6
- first_weight: bfloat16 [2048, 1024], P('chan', 'filt'), may hold values from -0.125 to 0.125
- group_weight: bfloat16 [3, 3, 32, 1024], P(None, None, None, 'filt'), may hold values from -0.375 to 0.375
- third_weight: bfloat16 [1024, 2048], P('chan', 'filt'), may hold values from -0.1875 to 0.1875
- out_grad: bfloat16 [16, 2048, 2048], P('rows', 'chan', 'filt'), may hold values from -6 to 6
Outputs:
- block_out: bfloat16 [16, 2048, 2048], P('rows', 'chan', 'filt')
- images_grad: float32 [16, 2048, 2048], P('rows', 'chan', 'filt')
- first_grad: float32 [2048, 1024], P('chan', 'filt')
- group_grad: float32 [3, 3, 32, 1024], P(None, None, None, 'filt')
- third_grad: float32 [1024, 2048], P('chan', 'filt')
The draws below stay inside these ranges and needn't reach their ends.
All inputs are finite; a program needn't handle non-finite values.
Results may differ from the reference program's by a relative error of at most 0.006.
Values may be sent and summed in bfloat16 or wider, within the bound.
A program may use at most 192 MiB of HBM per device.

```python
import jax
import jax.numpy as jnp
from jax import lax

C = 2048
MID = 1024
GS = 32
WD = 2048
H = 16
GROUPS = 32


def level_of(own_key, shape, split, low, top_value):
    def one(axis_at, blocks):
        draws = jax.random.uniform(jax.random.fold_in(jax.random.fold_in(own_key, 6), axis_at), (blocks,), jnp.float32, low / len(split), top_value / len(split))
        return jnp.repeat(jnp.exp(draws), shape[axis_at] // blocks).reshape((-1,) + (1,) * (len(shape) - axis_at - 1))

    loudness = one(*split[0])
    for cut in split[1:]:
        loudness = loudness * one(*cut)
    return loudness


def scatter_about(rng, shape, width, bound, shards=(), dtype=jnp.bfloat16):
    loudness = level_of(rng, shape, shards, -0.22, 0.18) if shards else 1.0
    values = jax.random.normal(rng, shape, jnp.float32) * width * loudness
    return jnp.minimum(jnp.maximum(values, -bound), bound).astype(dtype)


def setup_inputs(seed: int = 0) -> dict:
    arg_keys = jax.random.split(jax.random.key(seed), 6)
    return {
        "images": scatter_about(arg_keys[0], (H, WD, C), 1.0, 6.0, ((0, 4), (1, 2), (2, 4))),
        "first_weight": scatter_about(arg_keys[1], (C, MID), C ** -0.5, 0.125, ((0, 2), (1, 4))),
        "group_weight": scatter_about(arg_keys[2], (3, 3, GS, MID), (9 * GS) ** -0.5, 0.375, ((3, 4),)),
        "third_weight": scatter_about(arg_keys[3], (MID, C), MID ** -0.5, 0.1875, ((0, 2), (1, 4))),
        "out_grad": scatter_about(arg_keys[4], (H, WD, C), 1.0, 6.0, ((0, 4), (1, 2), (2, 4))),
    }


def silu_slope(values):
    logistic = jax.nn.sigmoid(values)
    return logistic * (1.0 + values * (1.0 - logistic))

def group_conv(values, kernel):
    result = lax.conv_general_dilated(values[None], kernel, (1, 1), 'SAME', dimension_numbers=('NHWC', 'HWIO', 'NHWC'), feature_group_count=GROUPS, precision=lax.Precision.HIGHEST)
    return result[0]

def reference(images, first_weight, group_weight, third_weight, out_grad):
    pixels = H * WD
    flat_images = images.reshape(pixels, C)
    pre_first = jnp.dot(flat_images, first_weight, preferred_element_type=jnp.float32)
    act_first = jax.nn.silu(pre_first).astype(jnp.bfloat16).reshape(H, WD, MID)
    kernel = group_weight.astype(jnp.float32)
    pre_group = group_conv(act_first.astype(jnp.float32), kernel)
    act_group = jax.nn.silu(pre_group).astype(jnp.bfloat16).reshape(pixels, MID)
    third_out = jnp.dot(act_group, third_weight, preferred_element_type=jnp.float32)
    block_out = (flat_images.astype(jnp.float32) + third_out).astype(jnp.bfloat16).reshape(H, WD, C)
    grad_flat = out_grad.reshape(pixels, C)
    mid_grad = lax.dot_general(grad_flat, third_weight, (((1,), (1,)), ((), ())), preferred_element_type=jnp.float32)
    third_grad = lax.dot_general(act_group, grad_flat, (((0,), (0,)), ((), ())), preferred_element_type=jnp.float32)
    group_delta = (mid_grad * silu_slope(pre_group.reshape(pixels, MID))).astype(jnp.bfloat16).reshape(H, WD, MID)
    unused, pullback = jax.vjp(group_conv, act_first.astype(jnp.float32), kernel)
    first_back, group_grad = pullback(group_delta.astype(jnp.float32))
    first_delta = (first_back.reshape(pixels, MID) * silu_slope(pre_first)).astype(jnp.bfloat16)
    first_grad = lax.dot_general(flat_images, first_delta, (((0,), (0,)), ((), ())), preferred_element_type=jnp.float32)
    back_images = lax.dot_general(first_delta, first_weight, (((1,), (1,)), ((), ())), preferred_element_type=jnp.float32)
    images_grad = (grad_flat.astype(jnp.float32) + back_images).reshape(H, WD, C)
    return (block_out, images_grad, first_grad, group_grad, third_grad)
```

```python
import jax
import jax.numpy as jnp
from jax import lax
from jax.experimental import pallas as pl
from jax.experimental.pallas import tpu as pltpu
from jax.sharding import PartitionSpec as P

BLOCK = 256
TAPS = [(a, b) for a in range(3) for b in range(3)]


def silu_slope(values):
    logistic = jax.nn.sigmoid(values)
    return logistic * (1.0 + values * (1.0 - logistic))


def to_pixels(block):
    count = lax.axis_size("filt")
    me = lax.axis_index("filt")
    rows, cols, chans = block.shape
    share = cols // count
    out = jnp.zeros((rows, share, chans * count), block.dtype)
    for step in range(count):
        target = lax.rem(me + step, count)
        piece = lax.dynamic_slice(block, (0, target * share, 0), (rows, share, chans))
        if step:
            piece = lax.ppermute(piece, "filt", [(i, (i + step) % count) for i in range(count)])
        source = lax.rem(me + count - step, count)
        out = lax.dynamic_update_slice(out, piece, (0, 0, source * chans))
    return out


def sent_back(block):
    count = lax.axis_size("filt")
    me = lax.axis_index("filt")
    rows, share, whole = block.shape
    chans = whole // count
    pieces = []
    for step in range(count):
        target = lax.rem(me + step, count)
        piece = lax.dynamic_slice(block, (0, 0, target * chans), (rows, share, chans))
        if step:
            piece = lax.ppermute(piece, "filt", [(i, (i + step) % count) for i in range(count)])
        pieces.append(piece)
    return pieces


def hold(pieces, step, *values):
    if step >= len(pieces):
        return values
    pieces[step], *values = lax.optimization_barrier((pieces[step], *values))
    return values


def placed(pieces):
    count = lax.axis_size("filt")
    me = lax.axis_index("filt")
    rows, share, chans = pieces[0].shape
    out = jnp.zeros((rows, share * count, chans), pieces[0].dtype)
    for step, piece in enumerate(pieces):
        source = lax.rem(me + count - step, count)
        out = lax.dynamic_update_slice(out, piece, (0, source * share, 0))
    return out


def whole_weight(shard):
    part = shard.shape[0] // lax.axis_size("rows")
    piece = lax.dynamic_slice_in_dim(shard, lax.axis_index("rows") * part, part, axis=0)
    piece = lax.all_gather(piece, "filt", axis=1, tiled=True)
    return lax.all_gather(piece, ("chan", "rows"), axis=0, tiled=True)


def summed_rows(partial):
    rows, chan = lax.axis_size("rows"), lax.axis_size("chan")
    part = partial.shape[0] // (rows * chan)
    split = partial.astype(jnp.bfloat16).reshape(chan, rows, part, partial.shape[1])
    split = split.swapaxes(0, 1).reshape(partial.shape)
    return lax.psum_scatter(split, "rows", scatter_dimension=0, tiled=True)


def column_windows(block):
    def edges(first, last, axis):
        count = lax.axis_size(axis)
        forward = [(i, i + 1) for i in range(count - 1)]
        backward = [(i + 1, i) for i in range(count - 1)]
        return lax.ppermute(last, axis, forward), lax.ppermute(first, axis, backward)

    low, high = edges(block[:1], block[-1:], "rows")
    tall = jnp.concatenate([low, block, high], axis=0)
    left, right = edges(tall[:, :1], tall[:, -1:], ("chan", "filt"))
    return (
        jnp.concatenate([left, tall[:, :-1]], axis=1),
        tall,
        jnp.concatenate([tall[:, 1:], right], axis=1),
    )


def block_kernels(kernel):
    group_size, mid = kernel.shape[2:]
    count = mid // BLOCK
    pieces = kernel.reshape(9, group_size, count, BLOCK).transpose(2, 0, 1, 3)
    tiled = jnp.tile(pieces, (1, 1, BLOCK // group_size, 1))
    group = jnp.arange(BLOCK) // group_size
    panels = jnp.where(group[:, None] == group[None, :], tiled, jnp.zeros_like(tiled))
    turned = panels.swapaxes(2, 3)
    return panels.reshape(count, 9 * BLOCK, BLOCK), turned.reshape(count, 9 * BLOCK, BLOCK)


def forward_kernel(s0, s1, s2, panel, pre_ref, act_ref):
    shifted = (s0, s1, s2)
    rows, cols = s0.shape[0] - 2, s0.shape[1]
    for i in range(rows):
        wide = jnp.concatenate([shifted[b][i + a] for a, b in TAPS], axis=1)
        pre = jnp.dot(wide, panel[0], preferred_element_type=jnp.float32)
        pre_ref[i * cols : (i + 1) * cols, :] = pre
        act_ref[i * cols : (i + 1) * cols, :] = jax.nn.silu(pre).astype(jnp.bfloat16)


def backward_kernel(group_size, s0, s1, s2, d0, d1, d2, panel, pre_ref, delta_ref, grad_ref):
    shifted, deltas = (s0, s1, s2), (d0, d1, d2)
    rows, cols = s0.shape[0] - 2, s0.shape[1]
    for i in range(rows):
        wide = jnp.concatenate([deltas[2 - b][i + 2 - a] for a, b in TAPS], axis=1)
        back = jnp.dot(wide, panel[0], preferred_element_type=jnp.float32)
        here = slice(i * cols, (i + 1) * cols)
        delta_ref[here, :] = (back * silu_slope(pre_ref[here, :])).astype(jnp.bfloat16)
    own = d1[1 : rows + 1].reshape(rows * cols, BLOCK).T
    out_group = lax.broadcasted_iota(jnp.int32, (BLOCK, BLOCK), 0) // group_size
    in_group = lax.broadcasted_iota(jnp.int32, (BLOCK, BLOCK), 1) // group_size
    same = out_group == in_group
    for tap, (a, b) in enumerate(TAPS):
        window = shifted[b][a : a + rows].reshape(rows * cols, BLOCK)
        full = jnp.dot(own, window, preferred_element_type=jnp.float32)
        full = jnp.where(same, full, 0.0)
        grad_ref[tap] = full.reshape(BLOCK // group_size, group_size, BLOCK).sum(axis=0)


def body(images, first_weight, group_weight, third_weight, out_grad):
    group_size = group_weight.shape[2]
    first_panel = whole_weight(first_weight)
    mid = first_panel.shape[1]
    count = mid // BLOCK
    image_pixels = to_pixels(images)
    rows, share, whole = image_pixels.shape
    pixels = rows * share
    out_grad_later, image_pixels = lax.optimization_barrier((out_grad, image_pixels))
    grad_pixels = to_pixels(out_grad_later)
    third_panel = whole_weight(third_weight)
    kernel = lax.all_gather(group_weight, "filt", axis=3, tiled=True)
    panels, turned = block_kernels(kernel)

    flat_images = image_pixels.reshape(pixels, whole)
    pre_first = jnp.dot(flat_images, first_panel, preferred_element_type=jnp.float32)
    act_first = jax.nn.silu(pre_first).astype(jnp.bfloat16).reshape(rows, share, mid)
    windows = column_windows(act_first)

    window_spec = pl.BlockSpec((rows + 2, share, BLOCK), lambda g: (0, 0, g))
    panel_spec = pl.BlockSpec((1, 9 * BLOCK, BLOCK), lambda g: (g, 0, 0))
    flat_spec = pl.BlockSpec((pixels, BLOCK), lambda g: (0, g))
    params = pltpu.CompilerParams(vmem_limit_bytes=40 * 1024 * 1024)
    pre_group, act_group = pl.pallas_call(
        forward_kernel,
        grid=(count,),
        out_shape=(
            jax.ShapeDtypeStruct((pixels, mid), jnp.float32),
            jax.ShapeDtypeStruct((pixels, mid), jnp.bfloat16),
        ),
        in_specs=[window_spec] * 3 + [panel_spec],
        out_specs=(flat_spec, flat_spec),
        compiler_params=params,
        cost_estimate=pl.CostEstimate(
            flops=18 * pixels * mid * BLOCK, bytes_accessed=40 * pixels * mid, transcendentals=0
        ),
    )(*windows, panels)

    third_out = jnp.dot(act_group, third_panel, preferred_element_type=jnp.float32)
    block_pixels = (flat_images.astype(jnp.float32) + third_out).astype(jnp.bfloat16)
    block_pixels, pre_group = lax.optimization_barrier((block_pixels, pre_group))
    block_pieces = sent_back(block_pixels.reshape(rows, share, whole))
    flat_grad = grad_pixels.reshape(pixels, whole)
    mid_grad = lax.dot_general(
        flat_grad, third_panel, (((1,), (1,)), ((), ())), preferred_element_type=jnp.float32
    )
    group_delta = (mid_grad * silu_slope(pre_group)).astype(jnp.bfloat16)
    (group_delta,) = hold(block_pieces, 1, group_delta)
    delta_windows = column_windows(group_delta.reshape(rows, share, mid))
    third_part = lax.dot_general(
        act_group, flat_grad, (((0,), (0,)), ((), ())), preferred_element_type=jnp.float32
    )
    third_sum = summed_rows(third_part).astype(jnp.float32)
    third_sum = lax.psum_scatter(third_sum, "chan", scatter_dimension=0, tiled=True)
    delta_windows = hold(block_pieces, 2, *delta_windows)

    first_delta, kernel_part = pl.pallas_call(
        lambda *refs: backward_kernel(group_size, *refs),
        grid=(count,),
        out_shape=(
            jax.ShapeDtypeStruct((pixels, mid), jnp.bfloat16),
            jax.ShapeDtypeStruct((9, group_size, mid), jnp.float32),
        ),
        in_specs=[window_spec] * 6 + [panel_spec, flat_spec],
        out_specs=(flat_spec, pl.BlockSpec((9, group_size, BLOCK), lambda g: (0, 0, g))),
        compiler_params=params,
        cost_estimate=pl.CostEstimate(
            flops=36 * pixels * mid * BLOCK, bytes_accessed=60 * pixels * mid, transcendentals=0
        ),
    )(*windows, *delta_windows, turned, pre_first)

    (first_delta,) = hold(block_pieces, 3, first_delta)
    block_out = placed(block_pieces)
    first_part = lax.dot_general(
        flat_images, first_delta, (((0,), (0,)), ((), ())), preferred_element_type=jnp.float32
    )
    back_pixels = lax.dot_general(
        first_delta, first_panel, (((1,), (1,)), ((), ())), preferred_element_type=jnp.float32
    ).astype(jnp.bfloat16)
    back_pieces = sent_back(back_pixels.reshape(rows, share, whole))
    kernel_sum = lax.psum_scatter(kernel_part, "filt", scatter_dimension=2, tiled=True)
    first_sum, third_sum, kernel_sum = hold(
        back_pieces, 1, summed_rows(first_part), third_sum, kernel_sum
    )
    first_sum = first_sum.astype(jnp.float32)
    first_sum = lax.psum_scatter(first_sum, "chan", scatter_dimension=0, tiled=True)
    third_sum = lax.psum_scatter(third_sum, "filt", scatter_dimension=1, tiled=True)
    kernel_sum = lax.psum(kernel_sum, ("rows", "chan"))
    first_sum, third_sum = hold(back_pieces, 2, first_sum, third_sum)
    first_sum = lax.psum_scatter(first_sum, "filt", scatter_dimension=1, tiled=True)
    third_grad = lax.all_gather(third_sum, "rows", axis=0, tiled=True)
    first_sum, kernel_sum = hold(back_pieces, 3, first_sum, kernel_sum)
    first_grad = lax.all_gather(first_sum, "rows", axis=0, tiled=True)
    back_images = placed(back_pieces)
    images_grad = out_grad.astype(jnp.float32) + back_images.astype(jnp.float32)

    own_mid = kernel_sum.shape[2]
    group_grad = kernel_sum.reshape(3, 3, group_size, own_mid // group_size, group_size)
    group_grad = group_grad.transpose(0, 1, 4, 3, 2).reshape(3, 3, group_size, own_mid)
    return (block_out, images_grad, first_grad, group_grad, third_grad)


def solution(mesh):
    in_specs = (
        P("rows", "chan", "filt"),
        P("chan", "filt"),
        P(None, None, None, "filt"),
        P("chan", "filt"),
        P("rows", "chan", "filt"),
    )
    out_specs = (
        P("rows", "chan", "filt"),
        P("rows", "chan", "filt"),
        P("chan", "filt"),
        P(None, None, None, "filt"),
        P("chan", "filt"),
    )
    return jax.shard_map(body, mesh=mesh, in_specs=in_specs, out_specs=out_specs, check_vma=False)
```

```python
import jax
import jax.numpy as jnp
from jax import lax
from jax.experimental import pallas as pl
from jax.experimental.pallas import tpu as pltpu
from jax.sharding import PartitionSpec as P

BLOCK = 256
TAPS = [(a, b) for a in range(3) for b in range(3)]


def silu_slope(values):
    logistic = jax.nn.sigmoid(values)
    return logistic * (1.0 + values * (1.0 - logistic))


def sent_pixels(block):
    count = lax.axis_size("filt")
    me = lax.axis_index("filt")
    rows, cols, chans = block.shape
    share = cols // count
    pieces = []
    for step in range(count):
        target = lax.rem(me + step, count)
        piece = lax.dynamic_slice(block, (0, target * share, 0), (rows, share, chans))
        if step:
            piece = lax.ppermute(piece, "filt", [(i, (i + step) % count) for i in range(count)])
        pieces.append(piece)
    return pieces


def all_channels(pieces):
    count = lax.axis_size("filt")
    me = lax.axis_index("filt")
    rows, share, chans = pieces[0].shape
    out = jnp.zeros((rows, share, chans * count), pieces[0].dtype)
    for step, piece in enumerate(pieces):
        source = lax.rem(me + count - step, count)
        out = lax.dynamic_update_slice(out, piece, (0, 0, source * chans))
    return out


def sent_back(block):
    count = lax.axis_size("filt")
    me = lax.axis_index("filt")
    rows, share, whole = block.shape
    chans = whole // count
    pieces = []
    for step in range(count):
        target = lax.rem(me + step, count)
        piece = lax.dynamic_slice(block, (0, 0, target * chans), (rows, share, chans))
        if step:
            piece = lax.ppermute(piece, "filt", [(i, (i + step) % count) for i in range(count)])
        pieces.append(piece)
    return pieces


def hold(pieces, step, *values):
    if step >= len(pieces):
        return values
    pieces[step], *values = lax.optimization_barrier((pieces[step], *values))
    return values


def placed(pieces):
    count = lax.axis_size("filt")
    me = lax.axis_index("filt")
    rows, share, chans = pieces[0].shape
    out = jnp.zeros((rows, share * count, chans), pieces[0].dtype)
    for step, piece in enumerate(pieces):
        source = lax.rem(me + count - step, count)
        out = lax.dynamic_update_slice(out, piece, (0, source * share, 0))
    return out


def weight_part(shard):
    part = shard.shape[0] // lax.axis_size("rows")
    piece = lax.dynamic_slice_in_dim(shard, lax.axis_index("rows") * part, part, axis=0)
    return lax.all_gather(piece, "filt", axis=1, tiled=True)


def chan_sum(values):
    if lax.axis_size("chan") != 2:
        return lax.psum_scatter(values, "chan", scatter_dimension=0, tiled=True)
    me, half = lax.axis_index("chan"), values.shape[0] // 2
    other = lax.dynamic_slice_in_dim(values, (1 - me) * half, half, axis=0)
    other = lax.ppermute(other, "chan", [(0, 1), (1, 0)])
    return lax.dynamic_slice_in_dim(values, me * half, half, axis=0) + other


def summed_rows(partial):
    rows, chan = lax.axis_size("rows"), lax.axis_size("chan")
    part = partial.shape[0] // (rows * chan)
    split = partial.astype(jnp.bfloat16).reshape(chan, rows, part, partial.shape[1])
    split = split.swapaxes(0, 1).reshape(partial.shape)
    return lax.psum_scatter(split, "rows", scatter_dimension=0, tiled=True)


def column_windows(block):
    def edges(first, last, axis):
        count = lax.axis_size(axis)
        forward = [(i, i + 1) for i in range(count - 1)]
        backward = [(i + 1, i) for i in range(count - 1)]
        return lax.ppermute(last, axis, forward), lax.ppermute(first, axis, backward)

    low, high = edges(block[:1], block[-1:], "rows")
    tall = jnp.concatenate([low, block, high], axis=0)
    left, right = edges(tall[:, :1], tall[:, -1:], ("chan", "filt"))
    return (
        jnp.concatenate([left, tall[:, :-1]], axis=1),
        tall,
        jnp.concatenate([tall[:, 1:], right], axis=1),
    )


def block_kernels(kernel):
    group_size, mid = kernel.shape[2:]
    count = mid // BLOCK
    pieces = kernel.reshape(9, group_size, count, BLOCK).transpose(2, 0, 1, 3)
    tiled = jnp.tile(pieces, (1, 1, BLOCK // group_size, 1))
    group = jnp.arange(BLOCK) // group_size
    panels = jnp.where(group[:, None] == group[None, :], tiled, jnp.zeros_like(tiled))
    turned = panels.swapaxes(2, 3)
    return panels.reshape(count, 9 * BLOCK, BLOCK), turned.reshape(count, 9 * BLOCK, BLOCK)


def forward_kernel(s0, s1, s2, panel, pre_ref, act_ref):
    shifted = (s0, s1, s2)
    rows, cols = s0.shape[0] - 2, s0.shape[1]
    for i in range(rows):
        wide = jnp.concatenate([shifted[b][i + a] for a, b in TAPS], axis=1)
        pre = jnp.dot(wide, panel[0], preferred_element_type=jnp.float32)
        pre_ref[i * cols : (i + 1) * cols, :] = pre
        act_ref[i * cols : (i + 1) * cols, :] = jax.nn.silu(pre).astype(jnp.bfloat16)


def backward_kernel(group_size, s0, s1, s2, d0, d1, d2, panel, pre_ref, delta_ref, grad_ref):
    shifted, deltas = (s0, s1, s2), (d0, d1, d2)
    rows, cols = s0.shape[0] - 2, s0.shape[1]
    for i in range(rows):
        wide = jnp.concatenate([deltas[2 - b][i + 2 - a] for a, b in TAPS], axis=1)
        back = jnp.dot(wide, panel[0], preferred_element_type=jnp.float32)
        here = slice(i * cols, (i + 1) * cols)
        delta_ref[here, :] = (back * silu_slope(pre_ref[here, :])).astype(jnp.bfloat16)
    own = d1[1 : rows + 1].reshape(rows * cols, BLOCK).T
    out_group = lax.broadcasted_iota(jnp.int32, (BLOCK, BLOCK), 0) // group_size
    in_group = lax.broadcasted_iota(jnp.int32, (BLOCK, BLOCK), 1) // group_size
    same = out_group == in_group
    for tap, (a, b) in enumerate(TAPS):
        window = shifted[b][a : a + rows].reshape(rows * cols, BLOCK)
        full = jnp.dot(own, window, preferred_element_type=jnp.float32)
        full = jnp.where(same, full, 0.0)
        grad_ref[tap] = full.reshape(BLOCK // group_size, group_size, BLOCK).sum(axis=0)


def body(images, first_weight, group_weight, third_weight, out_grad):
    group_size = group_weight.shape[2]
    image_pieces = sent_pixels(images)
    kernel = lax.all_gather(group_weight, "filt", axis=3, tiled=True)
    kernel, first_part, third_part = hold(
        image_pieces, 1, kernel, weight_part(first_weight), weight_part(third_weight)
    )
    first_panel = lax.all_gather(first_part, ("chan", "rows"), axis=0, tiled=True)
    mid = first_panel.shape[1]
    count = mid // BLOCK
    image_pixels = all_channels(image_pieces)
    rows, share, whole = image_pixels.shape
    pixels = rows * share
    out_grad_later, image_pixels = lax.optimization_barrier((out_grad, image_pixels))
    grad_pixels = all_channels(sent_pixels(out_grad_later))
    third_panel = lax.all_gather(third_part, ("chan", "rows"), axis=0, tiled=True)
    panels, turned = block_kernels(kernel)

    flat_images = image_pixels.reshape(pixels, whole)
    pre_first = jnp.dot(flat_images, first_panel, preferred_element_type=jnp.float32)
    act_first = jax.nn.silu(pre_first).astype(jnp.bfloat16).reshape(rows, share, mid)
    windows = column_windows(act_first)

    window_spec = pl.BlockSpec((rows + 2, share, BLOCK), lambda g: (0, 0, g))
    panel_spec = pl.BlockSpec((1, 9 * BLOCK, BLOCK), lambda g: (g, 0, 0))
    flat_spec = pl.BlockSpec((pixels, BLOCK), lambda g: (0, g))
    params = pltpu.CompilerParams(vmem_limit_bytes=40 * 1024 * 1024)
    pre_group, act_group = pl.pallas_call(
        forward_kernel,
        grid=(count,),
        out_shape=(
            jax.ShapeDtypeStruct((pixels, mid), jnp.float32),
            jax.ShapeDtypeStruct((pixels, mid), jnp.bfloat16),
        ),
        in_specs=[window_spec] * 3 + [panel_spec],
        out_specs=(flat_spec, flat_spec),
        compiler_params=params,
        cost_estimate=pl.CostEstimate(
            flops=18 * pixels * mid * BLOCK, bytes_accessed=40 * pixels * mid, transcendentals=0
        ),
    )(*windows, panels)

    third_out = jnp.dot(act_group, third_panel, preferred_element_type=jnp.float32)
    block_pixels = (flat_images.astype(jnp.float32) + third_out).astype(jnp.bfloat16)
    block_pixels, pre_group = lax.optimization_barrier((block_pixels, pre_group))
    block_pieces = sent_back(block_pixels.reshape(rows, share, whole))
    flat_grad = grad_pixels.reshape(pixels, whole)
    mid_grad = lax.dot_general(
        flat_grad, third_panel, (((1,), (1,)), ((), ())), preferred_element_type=jnp.float32
    )
    group_delta = (mid_grad * silu_slope(pre_group)).astype(jnp.bfloat16)
    (group_delta,) = hold(block_pieces, 1, group_delta)
    delta_windows = column_windows(group_delta.reshape(rows, share, mid))
    third_part = lax.dot_general(
        act_group, flat_grad, (((0,), (0,)), ((), ())), preferred_element_type=jnp.float32
    )
    *delta_windows, third_sum = hold(block_pieces, 2, *delta_windows, summed_rows(third_part))
    third_sum = chan_sum(third_sum.astype(jnp.float32))

    first_delta, kernel_part = pl.pallas_call(
        lambda *refs: backward_kernel(group_size, *refs),
        grid=(count,),
        out_shape=(
            jax.ShapeDtypeStruct((pixels, mid), jnp.bfloat16),
            jax.ShapeDtypeStruct((9, group_size, mid), jnp.float32),
        ),
        in_specs=[window_spec] * 6 + [panel_spec, flat_spec],
        out_specs=(flat_spec, pl.BlockSpec((9, group_size, BLOCK), lambda g: (0, 0, g))),
        compiler_params=params,
        cost_estimate=pl.CostEstimate(
            flops=36 * pixels * mid * BLOCK, bytes_accessed=60 * pixels * mid, transcendentals=0
        ),
    )(*windows, *delta_windows, turned, pre_first)

    first_delta, third_sum = hold(block_pieces, 3, first_delta, third_sum)
    third_sum = lax.psum_scatter(third_sum, "filt", scatter_dimension=1, tiled=True)
    block_out = placed(block_pieces)
    first_part = lax.dot_general(
        flat_images, first_delta, (((0,), (0,)), ((), ())), preferred_element_type=jnp.float32
    )
    back_pixels = lax.dot_general(
        first_delta, first_panel, (((1,), (1,)), ((), ())), preferred_element_type=jnp.float32
    ).astype(jnp.bfloat16)
    back_pieces = sent_back(back_pixels.reshape(rows, share, whole))
    kernel_sum = lax.psum_scatter(kernel_part, "filt", scatter_dimension=2, tiled=True)
    first_sum, third_sum = hold(back_pieces, 1, summed_rows(first_part), third_sum)
    first_sum = chan_sum(first_sum.astype(jnp.float32))
    third_grad = lax.all_gather(third_sum, "rows", axis=0, tiled=True)
    first_sum, kernel_sum = hold(back_pieces, 2, first_sum, kernel_sum)
    first_sum = lax.psum_scatter(first_sum, "filt", scatter_dimension=1, tiled=True)
    kernel_sum = lax.psum(kernel_sum, ("rows", "chan"))
    (first_sum,) = hold(back_pieces, 3, first_sum)
    first_grad = lax.all_gather(first_sum, "rows", axis=0, tiled=True)
    back_images = placed(back_pieces)
    images_grad = out_grad.astype(jnp.float32) + back_images.astype(jnp.float32)

    own_mid = kernel_sum.shape[2]
    group_grad = kernel_sum.reshape(3, 3, group_size, own_mid // group_size, group_size)
    group_grad = group_grad.transpose(0, 1, 4, 3, 2).reshape(3, 3, group_size, own_mid)
    return (block_out, images_grad, first_grad, group_grad, third_grad)


def solution(mesh):
    in_specs = (
        P("rows", "chan", "filt"),
        P("chan", "filt"),
        P(None, None, None, "filt"),
        P("chan", "filt"),
        P("rows", "chan", "filt"),
    )
    out_specs = (
        P("rows", "chan", "filt"),
        P("rows", "chan", "filt"),
        P("chan", "filt"),
        P(None, None, None, "filt"),
        P("chan", "filt"),
    )
    return jax.shard_map(body, mesh=mesh, in_specs=in_specs, out_specs=out_specs, check_vma=False)
```
